512 devices in a mesh: enc: 2 (over core), blk: 8 (over y_lo, x), voc: 32 (over z, y_hi).
Axes of the slice: x: 4, y: 4 (y_hi: 2, y_lo: 2; y = y_hi * 2 + y_lo), z: 16, core: 2. Of those that a mesh axis runs over, the one named last changes fastest.
Arguments:
- queries: bfloat16 [16384, 2048], P(('blk', 'voc'), 'enc'), may hold values from -100 to 100
- residual: bfloat16 [16384, 2048], P(('blk', 'voc'), 'enc'), may hold values from -6 to 6
- mem_keys: bfloat16 [8192, 2048], P(('blk', 'voc'), 'enc'), may hold values from -6 to 6
- mem_values: bfloat16 [8192, 2048], P(('blk', 'voc'), 'enc'), may hold values from -6 to 6
- dec_ids: int32 [16384], P(('blk', 'voc')), may hold values from 0 to 31, as said below
- mem_ids: int32 [8192], P(('blk', 'voc')), may hold values from 0 to 31, as said below
- targets: int32 [16384], P(('blk', 'voc')), may hold values from 0 to 32767
- ln_gain: float32 [2048], replicated, may hold values from 0.5 to 1.5
- ln_bias: float32 [2048], replicated, may hold values from -3 to 3
- head_weight: bfloat16 [2048, 32768], P(None, ('enc', 'voc')), may hold values from -1 to 1
Outputs:
- row_loss: float32 [16384], P(('blk', 'voc'))
The draws below stay inside these ranges and needn't reach their ends.
Inputs may be any that keep to these rules, and one draw needn't show every extreme that they name: `dec_ids`: within each block of 2048 decoder rows the numbers never fall, start at 0 and end at 31, and each of the 32 sentences has at least one row. `mem_ids`: within each block of 1024 memory rows the numbers never fall, start at 0 and end at 31, and each of the 32 sentences has at least one row.
All inputs are finite; a program needn't handle non-finite values.
Results may differ from the reference program's by a relative error of at most 0.003.
Values may be sent and summed in bfloat16 or wider, within the bound.
No kernel may reach another device: no remote copies, remote signals or barrier semaphores. Data moves between devices by JAX's collectives and lax.ppermute only.
A program may use at most 64 MiB of HBM per device.

```python
import math
import jax
import jax.numpy as jnp
import numpy as np
from jax import lax

D = 2048
HEADS = 16
SENT = 32
DEC_BLK = 2048
MEM_BLK = 1024
DEC_ROWS = 16384
MEM_ROWS = 8192
VOCAB = 32768
N_BLK = 8


def block_ids(key, length, total_rows, seg_count):
    blocks = total_rows // length

    def one_block(block_index):
        block_key = jax.random.fold_in(key, block_index)
        cut_points = jax.random.permutation(block_key, length - 1)[:seg_count - 1].astype(jnp.int32) + 1
        positions = jnp.arange(length, dtype=jnp.int32)
        return jnp.sum((cut_points[None, :] <= positions[:, None]).astype(jnp.int32), axis=1)
    return jax.vmap(one_block)(jnp.arange(blocks, dtype=jnp.int32)).reshape(total_rows).astype(jnp.int32)


def draw_dec_ids(key, part):
    key = jax.random.fold_in(key, 11)
    return block_ids(key, DEC_BLK, DEC_ROWS, SENT)


def draw_mem_ids(key, part):
    key = jax.random.fold_in(key, 23)
    return block_ids(key, MEM_BLK, MEM_ROWS, SENT)


def draw_queries(key, part):
    key = jax.random.fold_in(key, 37)
    value_key = jax.random.fold_in(key, 0)
    values = jnp.clip(jax.random.normal(value_key, (DEC_ROWS, D), jnp.float32), -4.0, 4.0)
    return values.astype(jnp.bfloat16)


def draw_head_weight(key, part):
    key = jax.random.fold_in(key, 53)
    value_key = jax.random.fold_in(key, 0)
    values = jnp.clip(jax.random.normal(value_key, (D, VOCAB), jnp.float32) / math.sqrt(D), -1.0, 1.0)
    return values.astype(jnp.bfloat16)


def place_ends(drawn, rng, low, high):
    shape = drawn.shape
    spot = [jax.random.randint(jax.random.fold_in(rng, axis), (), 0, shape[axis]) for axis in range(len(shape))]
    drawn = drawn.at[tuple(spot)].set(low)
    longest = shape.index(max(shape))
    spot[longest] = (spot[longest] + 1) % shape[longest]
    return drawn.at[tuple(spot)].set(high)


def block_scale(key, extent, cuts, least, top_value):
    gain = 1.0
    for axis_at, shards_of in cuts:
        heights = jax.random.uniform(jax.random.fold_in(jax.random.fold_in(key, 6), axis_at), (shards_of,), jnp.float32, least / len(cuts), top_value / len(cuts))
        gain = gain * jnp.repeat(jnp.exp(heights), extent[axis_at] // shards_of).reshape((-1,) + (1,) * (len(extent) - 1 - axis_at))
    return gain


def rank_bounds(count, lean):
    loads = [(1 << 20) // math.isqrt(standing ** lean) + 1 for standing in range(1, count + 1)]
    width = 1 + sum(loads) // (1 << 30)
    return np.cumsum(np.array([max(1, weight // width) for weight in loads]))


def ranked_ids(key, shape, count, slope):
    table = rank_bounds(count, slope)
    pick = jax.random.randint(jax.random.fold_in(key, 1), shape, 0, int(table[count - 1]))
    standing = jnp.searchsorted(jnp.asarray(table, jnp.int32), pick, side="right")
    return jax.random.permutation(jax.random.fold_in(key, 2), count)[standing].astype(jnp.int32)


def centred(key, dims, deviation, bound, cuts=(), held_as=jnp.bfloat16):
    entries = jax.random.normal(key, dims, jnp.float32) * deviation
    if len(cuts) > 0:
        entries = block_scale(key, dims, cuts, -0.22, 0.18) * entries
    return jnp.clip(entries, min=-bound, max=bound).astype(held_as)


def setup_inputs(seed: int = 0) -> dict:
    arg_keys = jax.random.split(jax.random.key(seed), 11)
    queries = draw_queries(jax.random.fold_in(arg_keys[10], 71), 0)
    residual = centred(arg_keys[1], (DEC_ROWS, D), 1.0, 6.0, ((0, 256), (1, 2)))
    mem_keys = centred(arg_keys[2], (MEM_ROWS, D), 1.0, 6.0, ((0, 256), (1, 2)))
    mem_values = centred(arg_keys[3], (MEM_ROWS, D), 1.0, 6.0, ((0, 256), (1, 2)))
    dec_ids = draw_dec_ids(jax.random.fold_in(arg_keys[10], 71), 0)
    mem_ids = draw_mem_ids(jax.random.fold_in(arg_keys[10], 71), 0)
    targets = place_ends(ranked_ids(arg_keys[6], (DEC_ROWS,), VOCAB, 2), jax.random.fold_in(arg_keys[6], 3), 0, VOCAB - 1).astype(jnp.int32)
    ln_gain = jnp.clip(1.0 + 0.1 * jax.random.normal(arg_keys[7], (D,), jnp.float32), 0.5, 1.5)
    ln_bias = centred(arg_keys[8], (D,), 0.5, 3.0, (), jnp.float32)
    head_weight = draw_head_weight(jax.random.fold_in(arg_keys[10], 71), 0)
    return {"queries": queries, "residual": residual, "mem_keys": mem_keys, "mem_values": mem_values, "dec_ids": dec_ids, "mem_ids": mem_ids, "targets": targets, "ln_gain": ln_gain, "ln_bias": ln_bias, "head_weight": head_weight}


EPS_SMOOTH = 0.1
Z_COEF = 0.0001
LN_EPS = 1e-05

def attend_block(pieces):
    block_q, block_k, block_v, block_dec, block_mem = pieces
    head_dim = D // HEADS
    query_heads = block_q.astype(jnp.float32).reshape(block_q.shape[0], HEADS, head_dim)
    key_heads = block_k.astype(jnp.float32).reshape(block_k.shape[0], HEADS, head_dim)
    value_heads = block_v.astype(jnp.float32).reshape(block_v.shape[0], HEADS, head_dim)
    scores = jnp.einsum('ihd,jhd->hij', query_heads, key_heads) * (1.0 / math.sqrt(head_dim))
    allowed = block_dec[:, None] == block_mem[None, :]
    scores = jnp.where(allowed[None], scores, -jnp.inf)
    top_score = lax.optimization_barrier(jnp.max(scores, axis=2, keepdims=True))
    raised = jnp.exp(scores - top_score)
    weights = (raised / lax.optimization_barrier(jnp.sum(raised, axis=2, keepdims=True))).astype(jnp.bfloat16)
    weights = lax.optimization_barrier(weights).astype(jnp.float32)
    context = jnp.einsum('hij,jhd->ihd', weights, value_heads)
    return context.reshape(block_q.shape[0], D).astype(jnp.bfloat16)

def reference(queries, residual, mem_keys, mem_values, dec_ids, mem_ids, targets, ln_gain, ln_bias, head_weight):
    context = lax.map(attend_block, (queries.reshape(N_BLK, DEC_BLK, D), mem_keys.reshape(N_BLK, MEM_BLK, D), mem_values.reshape(N_BLK, MEM_BLK, D), dec_ids.reshape(N_BLK, DEC_BLK), mem_ids.reshape(N_BLK, MEM_BLK))).reshape(DEC_ROWS, D)
    context = lax.optimization_barrier(context)
    summed = (residual.astype(jnp.float32) + context.astype(jnp.float32)).astype(jnp.bfloat16)
    summed = lax.optimization_barrier(summed).astype(jnp.float32)
    row_mean = lax.optimization_barrier(jnp.mean(summed, axis=1, keepdims=True))
    centered = summed - row_mean
    row_var = lax.optimization_barrier(jnp.mean(centered * centered, axis=1, keepdims=True))
    normed = (centered * lax.rsqrt(row_var + LN_EPS) * ln_gain + ln_bias).astype(jnp.bfloat16)
    row_block = math.gcd(512, DEC_ROWS)

    def head_block(pieces):
        block_rows, block_targets = pieces
        logits = jnp.dot(block_rows, head_weight, preferred_element_type=jnp.float32)
        top_logit = lax.optimization_barrier(jnp.max(logits, axis=1))
        exp_total = lax.optimization_barrier(jnp.sum(jnp.exp(logits - top_logit[:, None]), axis=1))
        log_total = top_logit + jnp.log(exp_total)
        positions = lax.broadcasted_iota(jnp.int32, logits.shape, 1)
        picked = lax.optimization_barrier(jnp.sum(jnp.where(positions == block_targets[:, None], logits, 0.0), axis=1))
        logit_mean = lax.optimization_barrier(jnp.sum(logits, axis=1)) / VOCAB
        return (1.0 - EPS_SMOOTH) * (log_total - picked) + EPS_SMOOTH * (log_total - logit_mean) + Z_COEF * log_total * log_total
    row_loss = lax.map(head_block, (normed.reshape(-1, row_block, D), targets.reshape(-1, row_block)))
    return row_loss.reshape(DEC_ROWS)
```

```python
import math

import jax
import jax.numpy as jnp
from jax import lax
from jax.experimental import pallas as pl
from jax.experimental.pallas import tpu as pltpu
from jax.sharding import Mesh
from jax.sharding import PartitionSpec as P

D = 2048
HEADS = 16
HEAD_DIM = D // HEADS

EPS_SMOOTH = 0.1
Z_COEF = 0.0001
LN_EPS = 1e-05

BF16 = jnp.bfloat16
F32 = jnp.float32

VOC = ("z", "yhi")


def attend_kernel(q_ref, r_ref, k_ref, v_ref, dec_ref, mem_ref, out_ref):
    scores = lax.dot_general(
        q_ref[...], k_ref[...], (((1,), (1,)), ((), ())), preferred_element_type=F32
    )
    scores = scores * (1.0 / math.sqrt(HEAD_DIM))
    scores = jnp.where(dec_ref[...] == mem_ref[...], scores, -jnp.inf)
    top = jnp.max(scores, axis=1, keepdims=True)
    raised = jnp.exp(scores - top)
    weights = (raised / jnp.sum(raised, axis=1, keepdims=True)).astype(BF16)
    context = jnp.dot(weights, v_ref[...], preferred_element_type=F32).astype(BF16)
    out_ref[...] = (r_ref[...].astype(F32) + context.astype(F32)).astype(BF16)


def attend(q, r, k, v, dec, mem):
    rows, mem_rows = q.shape[0], k.shape[0]
    tile = 128
    whole = lambda i: (0, 0)
    step = lambda i: (i, 0)
    return pl.pallas_call(
        attend_kernel,
        grid=(rows // tile,),
        in_specs=[
            pl.BlockSpec((tile, HEAD_DIM), step),
            pl.BlockSpec((tile, HEAD_DIM), step),
            pl.BlockSpec((mem_rows, HEAD_DIM), whole),
            pl.BlockSpec((mem_rows, HEAD_DIM), whole),
            pl.BlockSpec((tile, 1), step),
            pl.BlockSpec((1, mem_rows), whole),
        ],
        out_specs=pl.BlockSpec((tile, HEAD_DIM), step),
        out_shape=jax.ShapeDtypeStruct((rows, HEAD_DIM), BF16),
        compiler_params=pltpu.CompilerParams(vmem_limit_bytes=24 * 1024 * 1024),
        name="attend",
    )(q, r, k, v, dec, mem)


def head_kernel(vocab, starts_ref, x_ref, gain_ref, bias_ref, t_ref, w0_ref, w1_ref, out_ref, normed):
    heads, halves = x_ref.shape[0], x_ref.shape[2]
    chunk = x_ref.shape[-1]
    total = 0.0
    for half in range(halves):
        for head in range(heads):
            total = total + x_ref[head, 0, half].astype(F32)
    mean = jnp.sum(total, axis=1, keepdims=True) * (1.0 / D)
    square = 0.0
    for half in range(halves):
        for head in range(heads):
            centered = x_ref[head, 0, half].astype(F32) - mean
            square = square + centered * centered
    scale = lax.rsqrt(jnp.sum(square, axis=1, keepdims=True) * (1.0 / D) + LN_EPS)
    for half in range(halves):
        for head in range(heads):
            at = pl.ds((half * heads + head) * chunk, chunk)
            centered = x_ref[head, 0, half].astype(F32) - mean
            normed[:, at] = (centered * scale * gain_ref[:, at] + bias_ref[:, at]).astype(BF16)
    logits = [
        jnp.dot(normed[...], w_ref[...], preferred_element_type=F32) for w_ref in (w0_ref, w1_ref)
    ]
    top = jnp.maximum(
        jnp.max(logits[0], axis=1, keepdims=True), jnp.max(logits[1], axis=1, keepdims=True)
    )
    exps = sums = picks = 0.0
    for index, part in enumerate(logits):
        exps = exps + jnp.sum(jnp.exp(part - top), axis=1, keepdims=True)
        sums = sums + jnp.sum(part, axis=1, keepdims=True)
        column = lax.broadcasted_iota(jnp.int32, part.shape, 1) + starts_ref[index]
        picks = picks + jnp.sum(jnp.where(column == t_ref[...], part, 0.0), axis=1, keepdims=True)
    lse = top + jnp.log(exps)
    line = (1.0 - EPS_SMOOTH) * picks + (EPS_SMOOTH / vocab) * sums
    lane = lax.broadcasted_iota(jnp.int32, (lse.shape[0], 2), 1)
    out_ref[...] = jnp.where(lane == 0, lse, line)


def head_stats(x, gain, bias, targets, w0, w1, starts, vocab):
    heads, sets, halves, rows, chunk = x.shape
    tile = 128
    tiles = rows // tile
    whole = lambda i, s: (0, 0)
    spec = pltpu.PrefetchScalarGridSpec(
        num_scalar_prefetch=1,
        grid=(sets * tiles,),
        in_specs=[
            pl.BlockSpec(
                (heads, 1, halves, tile, chunk), lambda i, s: (0, i // tiles, 0, i % tiles, 0)
            ),
            pl.BlockSpec((1, D), whole),
            pl.BlockSpec((1, D), whole),
            pl.BlockSpec((tile, 1), lambda i, s: (i, 0)),
            pl.BlockSpec(w0.shape, whole),
            pl.BlockSpec(w1.shape, whole),
        ],
        out_specs=pl.BlockSpec((tile, 2), lambda i, s: (i, 0)),
        scratch_shapes=[pltpu.VMEM((tile, D), BF16)],
    )

    def kernel(*refs):
        head_kernel(vocab, *refs)

    return pl.pallas_call(
        kernel,
        grid_spec=spec,
        out_shape=jax.ShapeDtypeStruct((sets * rows, 2), F32),
        compiler_params=pltpu.CompilerParams(vmem_limit_bytes=40 * 1024 * 1024),
        name="head_stats",
    )(starts, x, gain, bias, targets, w0, w1)


def per_device(
    queries,
    residual,
    mem_keys,
    mem_values,
    dec_ids,
    mem_ids,
    targets,
    ln_gain,
    ln_bias,
    head_weight,
):
    enc, z, yhi = lax.axis_index("enc"), lax.axis_index("z"), lax.axis_index("yhi")
    z_count, y_count = lax.axis_size("z"), lax.axis_size("yhi")
    voc_count = z_count * y_count
    heads = queries.shape[1] // HEAD_DIM
    parts = voc_count // heads
    sets = parts // y_count
    rows, mem_rows = queries.shape[0], mem_keys.shape[0]
    piece = rows // parts
    width = head_weight.shape[1]
    vocab = width * voc_count * lax.axis_size("enc")

    with jax.named_scope("pack"):
        to_all = lambda a: jnp.broadcast_to(
            a.reshape(mem_rows, heads, 1, HEAD_DIM).transpose(1, 2, 0, 3),
            (heads, parts, mem_rows, HEAD_DIM),
        )
        to_part = lambda a: a.reshape(parts, piece, heads, HEAD_DIM).transpose(2, 0, 1, 3)
        dec_parts = dec_ids.reshape(parts, piece)
        target_sets = targets.reshape(sets, y_count, piece).transpose(1, 0, 2).reshape(y_count, -1)
        target_parts = jnp.broadcast_to(target_sets[None], (sets,) + target_sets.shape).reshape(
            parts, sets * piece
        )
        notes = jnp.concatenate(
            [
                dec_parts,
                jnp.broadcast_to(mem_ids[None], (parts, mem_rows)),
                target_parts // 256,
                target_parts % 256,
            ],
            axis=1,
        ).astype(BF16)
        notes = jnp.pad(notes, ((0, 0), (0, HEAD_DIM - notes.shape[1])))
        notes = jnp.broadcast_to(
            jnp.pad(notes[None, :, None], ((0, 0), (0, 0), (0, 7), (0, 0))),
            (heads, parts, 8, HEAD_DIM),
        )
        message = jnp.concatenate(
            [to_all(mem_keys), to_all(mem_values), to_part(queries), to_part(residual), notes],
            axis=2,
        ).reshape(voc_count, -1, HEAD_DIM)
    with jax.named_scope("spread"):
        got = lax.all_to_all(message, VOC, 0, 0, tiled=True)
    got, head_weight = lax.optimization_barrier((got, head_weight))
    with jax.named_scope("weights"):
        swap = [(0, 1), (1, 0)]
        weight_other = lax.ppermute(head_weight, "yhi", swap)

    with jax.named_scope("attention"):
        at_q = 2 * mem_rows
        take = lambda low, count: got[:, low : low + count].reshape(-1, HEAD_DIM)
        noted = got[:, at_q + 2 * piece].astype(jnp.int32)
        dec = noted[:, :piece].reshape(-1, 1)
        mem = noted[:, piece : piece + mem_rows].reshape(1, -1)
        at_t = piece + mem_rows
        target = (
            noted[:, at_t : at_t + sets * piece] * 256
            + noted[:, at_t + sets * piece : at_t + 2 * sets * piece]
        )
        target = target.reshape(voc_count, sets, piece).transpose(1, 0, 2).reshape(-1, 1)
        summed = attend(
            take(at_q, piece),
            take(at_q + piece, piece),
            take(0, mem_rows),
            take(mem_rows, mem_rows),
            dec,
            mem,
        )
    with jax.named_scope("rows"):
        full = lax.all_gather(summed, ("z", "enc"), axis=0)
        full = full.reshape((heads, sets, lax.axis_size("enc")) + summed.shape)
    with jax.named_scope("head"):
        slab = (enc * voc_count + z * y_count) * width
        starts = jnp.stack([slab + yhi * width, slab + (1 - yhi) * width]).astype(jnp.int32)
        stats = head_stats(
            full,
            ln_gain[None],
            ln_bias[None],
            target,
            head_weight,
            weight_other,
            starts,
            vocab,
        )
    with jax.named_scope("merge"):
        enc_count = lax.axis_size("enc")
        stats = stats.reshape(sets, voc_count, piece, 2).transpose(1, 3, 0, 2)
        stats = stats.reshape(voc_count, 2, sets * piece)
        stats = jnp.broadcast_to(stats[None], (enc_count,) + stats.shape)
        stats = stats.reshape(enc_count * voc_count, 2, sets * piece)
        merged = lax.all_to_all(stats, ("enc",) + VOC, 0, 0, tiled=True)
        merged = merged.reshape(enc_count * z_count, y_count, 2, sets * piece)
        lse, line = merged[:, :, 0], merged[:, :, 1]
        top = jnp.max(lse, axis=0)
        log_total = top + jnp.log(jnp.sum(jnp.exp(lse - top), axis=0))
        loss = log_total - jnp.sum(line, axis=0) + Z_COEF * log_total * log_total
        return loss.reshape(y_count, sets, piece).transpose(1, 0, 2).reshape(rows)


def solution(mesh):
    shape = dict(mesh.shape)
    fine = Mesh(
        mesh.devices.reshape(shape["enc"], shape["blk"], shape["voc"] // 2, 2),
        ("enc", "blk", "z", "yhi"),
    )
    held = ("blk",) + VOC
    in_specs = (
        P(held, "enc"),
        P(held, "enc"),
        P(held, "enc"),
        P(held, "enc"),
        P(held),
        P(held),
        P(held),
        P(),
        P(),
        P(None, ("enc",) + VOC),
    )
    return jax.shard_map(
        per_device, mesh=fine, in_specs=in_specs, out_specs=P(held), check_vma=False
    )
```

```python
import math

import jax
import jax.numpy as jnp
from jax import lax
from jax.experimental import pallas as pl
from jax.experimental.pallas import tpu as pltpu
from jax.sharding import Mesh
from jax.sharding import PartitionSpec as P

D = 2048
HEADS = 16
HEAD_DIM = D // HEADS

EPS_SMOOTH = 0.1
Z_COEF = 0.0001
LN_EPS = 1e-05

BF16 = jnp.bfloat16
F32 = jnp.float32
MIB = 1024 * 1024

VOC = ("z", "yhi")
SWAP = [(0, 1), (1, 0)]
EARLY_SHARE = 14 / 32


def pack_kernel(parts, q_ref, r_ref, k_ref, v_ref, out_ref):
    mem_rows = k_ref.shape[0]
    piece = q_ref.shape[0] // parts
    at_q = 2 * mem_rows
    for head in range(q_ref.shape[1] // HEAD_DIM):
        lanes = pl.ds(head * HEAD_DIM, HEAD_DIM)
        for part in range(parts):
            to = head * parts + part
            rows = pl.ds(part * piece, piece)
            out_ref[to, pl.ds(0, mem_rows)] = k_ref[:, lanes]
            out_ref[to, pl.ds(mem_rows, mem_rows)] = v_ref[:, lanes]
            out_ref[to, pl.ds(at_q, piece)] = q_ref[rows, lanes]
            out_ref[to, pl.ds(at_q + piece, piece)] = r_ref[rows, lanes]


def pack(q, r, k, v, parts):
    heads = q.shape[1] // HEAD_DIM
    depth = 2 * k.shape[0] + 2 * (q.shape[0] // parts)

    def kernel(*refs):
        pack_kernel(parts, *refs)

    return pl.pallas_call(
        kernel,
        out_shape=jax.ShapeDtypeStruct((heads * parts, depth, HEAD_DIM), BF16),
        compiler_params=pltpu.CompilerParams(vmem_limit_bytes=16 * MIB),
        name="pack",
    )(q, r, k, v)


def attend_kernel(piece, q_ref, r_ref, k_ref, v_ref, dec_ref, mem_ref, out_ref):
    scores = lax.dot_general(
        q_ref[...], k_ref[...], (((1,), (1,)), ((), ())), preferred_element_type=F32
    )
    scores = scores * (1.0 / math.sqrt(HEAD_DIM))
    scores = jnp.where(dec_ref[...] == mem_ref[...], scores, -jnp.inf)
    top = jnp.max(scores, axis=1, keepdims=True)
    raised = jnp.exp(scores - top)
    weights = (raised / jnp.sum(raised, axis=1, keepdims=True)).astype(BF16)
    context = jnp.dot(weights, v_ref[...], preferred_element_type=F32).astype(BF16)
    summed = r_ref[...].astype(F32) + context.astype(F32)
    halves = out_ref.shape[0]
    summed = summed.reshape(-1, halves, piece // halves, HEAD_DIM)
    for half in range(halves):
        out_ref[half] = summed[:, half].reshape(-1, HEAD_DIM).astype(BF16)


def attend(q, r, k, v, dec, mem, piece, halves):
    rows, mem_rows = q.shape[0], k.shape[0]
    tile = 128
    whole = lambda i: (0, 0)
    step = lambda i: (i, 0)

    def kernel(*refs):
        attend_kernel(piece, *refs)

    return pl.pallas_call(
        kernel,
        grid=(rows // tile,),
        in_specs=[
            pl.BlockSpec((tile, HEAD_DIM), step),
            pl.BlockSpec((tile, HEAD_DIM), step),
            pl.BlockSpec((mem_rows, HEAD_DIM), whole),
            pl.BlockSpec((mem_rows, HEAD_DIM), whole),
            pl.BlockSpec((tile, 1), step),
            pl.BlockSpec((1, mem_rows), whole),
        ],
        out_specs=pl.BlockSpec((halves, tile // halves, HEAD_DIM), lambda i: (0, i, 0)),
        out_shape=jax.ShapeDtypeStruct((halves, rows // halves, HEAD_DIM), BF16),
        compiler_params=pltpu.CompilerParams(vmem_limit_bytes=24 * MIB),
        name="attend",
    )(q, r, k, v, dec, mem)


def head_kernel(vocab, info_ref, x_ref, gain_ref, bias_ref, t_ref, *rest):
    slabs = len(rest) - 5
    w_refs = rest[:slabs]
    out_ref, held, normed, logits, sems = rest[slabs:]
    copies = [
        pltpu.make_async_copy(w_refs[k], held.at[k], sems.at[k]) for k in range(slabs)
    ]
    for copy in copies:
        copy.start()
    heads, sets, halves, rows, chunk = x_ref.shape
    mine = info_ref[slabs]
    step = 16
    for group in range(sets):
        for low in range(0, rows, step):
            at = pl.ds(low, step)
            parts = [
                x_ref[head, group, half, at].astype(F32)
                for half in range(halves)
                for head in range(heads)
            ]
            mean = jnp.sum(sum(parts[1:], parts[0]), axis=1, keepdims=True) * (1.0 / D)
            parts = [part - mean for part in parts]
            squares = [part * part for part in parts]
            var = jnp.sum(sum(squares[1:], squares[0]), axis=1, keepdims=True) * (1.0 / D)
            scale = lax.rsqrt(var + LN_EPS)
            for half in range(halves):
                base = jnp.where(mine == 0, half, 1 - half) * (heads * chunk)
                for head in range(heads):
                    lanes = pl.ds(pl.multiple_of(base + head * chunk, chunk), chunk)
                    value = parts[half * heads + head] * scale * gain_ref[:, lanes]
                    normed[pl.ds(group * rows + low, step), lanes] = (
                        value + bias_ref[:, lanes]
                    ).astype(BF16)
    total = sets * rows
    width = held.shape[2]
    for k in range(slabs):
        copies[k].wait()
        logits[:, pl.ds(k * width, width)] = jnp.dot(
            normed[...], held[k], preferred_element_type=F32
        )
    lane = lax.broadcasted_iota(jnp.int32, (step, 128), 1)
    for low in range(0, total, step):
        at = pl.ds(low, step)
        target = t_ref[at]
        top = logits[at, pl.ds(0, 128)]
        for col in range(128, slabs * width, 128):
            top = jnp.maximum(top, logits[at, pl.ds(col, 128)])
        top = jnp.max(top, axis=1, keepdims=True)
        exps = sums = picks = jnp.zeros((step, 128), F32)
        for k in range(slabs):
            offset = target - info_ref[k]
            for col in range(0, width, 128):
                part = logits[at, pl.ds(k * width + col, 128)]
                exps = exps + jnp.exp(part - top)
                sums = sums + part
                picks = picks + jnp.where(lane == offset - col, part, 0.0)
        lse = top + jnp.log(jnp.sum(exps, axis=1, keepdims=True))
        line = (1.0 - EPS_SMOOTH) * picks + (EPS_SMOOTH / vocab) * sums
        line = jnp.sum(line, axis=1, keepdims=True)
        pair = lax.broadcasted_iota(jnp.int32, (step, 2), 1)
        out_ref[at] = jnp.where(pair == 0, lse, line)


def head_stats(x, gain, bias, targets, slabs, info, vocab):
    heads, sets, halves, rows, chunk = x.shape
    total = sets * rows
    width = slabs[0].shape[1]

    def kernel(*refs):
        head_kernel(vocab, *refs)

    vmem = pl.BlockSpec(memory_space=pltpu.VMEM)
    return pl.pallas_call(
        kernel,
        in_specs=[pl.BlockSpec(memory_space=pltpu.SMEM), vmem, vmem, vmem, vmem]
        + [pl.BlockSpec(memory_space=pl.ANY)] * len(slabs),
        out_specs=vmem,
        out_shape=jax.ShapeDtypeStruct((total, 2), F32),
        scratch_shapes=[
            pltpu.VMEM((len(slabs), D, width), BF16),
            pltpu.VMEM((total, D), BF16),
            pltpu.VMEM((total, len(slabs) * width), F32),
            pltpu.SemaphoreType.DMA((len(slabs),)),
        ],
        compiler_params=pltpu.CompilerParams(vmem_limit_bytes=40 * MIB),
        name="head_stats",
    )(info, x, gain, bias, targets, *slabs)


def per_device(
    queries,
    residual,
    mem_keys,
    mem_values,
    dec_ids,
    mem_ids,
    targets,
    ln_gain,
    ln_bias,
    head_weight,
):
    enc, z, yhi = lax.axis_index("enc"), lax.axis_index("z"), lax.axis_index("yhi")
    enc_count, z_count, y_count = (lax.axis_size(name) for name in ("enc", "z", "yhi"))
    voc_count = z_count * y_count
    heads = queries.shape[1] // HEAD_DIM
    parts = voc_count // heads
    sets = parts // y_count
    rows, mem_rows = queries.shape[0], mem_keys.shape[0]
    piece = rows // parts
    slice_rows = piece // enc_count
    width = head_weight.shape[1]
    vocab = width * voc_count * enc_count

    with jax.named_scope("pack"):
        message = pack(queries, residual, mem_keys, mem_values, parts)
        first = jnp.concatenate([dec_ids, mem_ids, jnp.zeros((128 - rows - mem_rows,), jnp.int32)])
        second = jnp.concatenate([targets // 256, targets % 256])
        notes = jnp.stack([first, second]).astype(BF16)
        notes = jnp.broadcast_to(jnp.pad(notes, ((0, 6), (0, 0)))[None], (voc_count, 8, HEAD_DIM))
        message = jnp.concatenate([message, notes], axis=1)
    with jax.named_scope("spread"):
        got = lax.all_to_all(message, VOC, 0, 0, tiled=True)
    got, head_weight = lax.optimization_barrier((got, head_weight))
    with jax.named_scope("weights"):
        weight_y = lax.ppermute(head_weight, "yhi", SWAP)
        weight_e = lax.ppermute(head_weight, "enc", SWAP)
        weight_ye = lax.ppermute(weight_y, "enc", SWAP)

    with jax.named_scope("attention"):
        at_q = 2 * mem_rows
        take = lambda low, count: got[:, low : low + count].reshape(-1, HEAD_DIM)
        noted = got[:, at_q + 2 * piece : at_q + 2 * piece + 2].astype(jnp.int32)
        dec = lax.dynamic_slice_in_dim(
            noted[:, 0], ((z % sets) * y_count + yhi) * piece, piece, 1
        ).reshape(-1, 1)
        mem = noted[:, 0, rows : rows + mem_rows].reshape(1, -1)
        target = noted[:, 1, :rows] * 256 + noted[:, 1, rows:]
        target = target.reshape(voc_count, sets, y_count * enc_count, slice_rows)
        target = lax.dynamic_index_in_dim(target, yhi * enc_count + enc, 2, False)
        target = target.transpose(1, 0, 2)
        halves = attend(
            take(at_q, piece),
            take(at_q + piece, piece),
            take(0, mem_rows),
            take(mem_rows, mem_rows),
            dec,
            mem,
            piece,
            enc_count,
        )
    with jax.named_scope("halves"):
        kept = lax.dynamic_index_in_dim(halves, enc, 0, False)
        handed = lax.ppermute(
            lax.dynamic_index_in_dim(halves, 1 - enc, 0, False), "enc", SWAP
        )
        shard = jnp.stack([kept, handed])
    early = int(voc_count * EARLY_SHARE)
    slab = lambda e, y: ((e * voc_count) + z * y_count + y) * width
    info = jnp.stack(
        [slab(enc, yhi), slab(1 - enc, yhi), slab(enc, 1 - yhi), slab(1 - enc, 1 - yhi), enc]
    ).astype(jnp.int32)
    found = []
    for low, high in ((early, voc_count), (0, early)):
        with jax.named_scope("rows"):
            full = lax.all_gather(shard[:, low * slice_rows : high * slice_rows], "z", axis=0)
            full = full.reshape((heads, sets) + full.shape[1:])
        with jax.named_scope("head"):
            stats = head_stats(
                full,
                ln_gain[None],
                ln_bias[None],
                target[:, low:high].reshape(-1, 1),
                (head_weight, weight_e, weight_y, weight_ye),
                info,
                vocab,
            )
            found.append(stats.reshape(sets, high - low, slice_rows, 2))
    with jax.named_scope("merge"):
        stats = jnp.concatenate(found[::-1], axis=1).transpose(1, 3, 0, 2)
        stats = jnp.broadcast_to(
            stats.reshape(1, voc_count, 2, -1), (enc_count, voc_count, 2, sets * slice_rows)
        )
        merged = lax.all_to_all(
            stats.reshape(enc_count * voc_count, 2, -1), ("enc",) + VOC, 0, 0, tiled=True
        )
        merged = merged.reshape(enc_count, z_count, y_count, 2, sets, slice_rows)
        lse, line = merged[:, :, :, 0], merged[:, :, :, 1]
        top = jnp.max(lse, axis=1, keepdims=True)
        log_total = top[:, 0] + jnp.log(jnp.sum(jnp.exp(lse - top), axis=1))
        loss = log_total - jnp.sum(line, axis=1) + Z_COEF * log_total * log_total
        return loss.transpose(2, 1, 0, 3).reshape(rows)


def solution(mesh):
    shape = dict(mesh.shape)
    fine = Mesh(
        mesh.devices.reshape(shape["enc"], shape["blk"], shape["voc"] // 2, 2),
        ("enc", "blk", "z", "yhi"),
    )
    held = ("blk",) + VOC
    in_specs = (
        P(held, "enc"),
        P(held, "enc"),
        P(held, "enc"),
        P(held, "enc"),
        P(held),
        P(held),
        P(held),
        P(),
        P(),
        P(None, ("enc",) + VOC),
    )
    return jax.shard_map(
        per_device, mesh=fine, in_specs=in_specs, out_specs=P(held), check_vma=False
    )
```

```python
import math

import jax
import jax.numpy as jnp
from jax import lax
from jax.experimental import pallas as pl
from jax.experimental.pallas import tpu as pltpu
from jax.sharding import Mesh
from jax.sharding import PartitionSpec as P

D = 2048
HEADS = 16
HEAD_DIM = D // HEADS

EPS_SMOOTH = 0.1
Z_COEF = 0.0001
LN_EPS = 1e-05

BF16 = jnp.bfloat16
F32 = jnp.float32
MIB = 1024 * 1024

VOC = ("zh", "zl", "yhi")
SWAP = [(0, 1), (1, 0)]
CROSS = [(0, 3), (3, 0), (1, 2), (2, 1)]
EARLY_SHARE = 14 / 32


def pack_kernel(parts, *refs):
    sources, out_ref, (q, r, k, v, dec, mem, target), sems = (
        refs[:7],
        refs[7],
        refs[8:15],
        refs[15],
    )
    held = (q, r, k, v, dec, mem, target)
    copies = [
        pltpu.make_async_copy(source, buffer, sems.at[index])
        for index, (source, buffer) in enumerate(zip(sources, held))
    ]
    for copy in copies:
        copy.start()
    for copy in copies:
        copy.wait()
    mem_rows = k.shape[0]
    rows = q.shape[0]
    piece = rows // parts
    at_q = 2 * mem_rows
    note_rows = out_ref.shape[1] - at_q - 2 * piece
    wide = lambda a: jnp.pad(a.astype(F32), ((0, 0), (0, HEAD_DIM - a.shape[1])))
    row = lax.broadcasted_iota(jnp.int32, (note_rows, HEAD_DIM), 0)
    notes = jnp.zeros((note_rows, HEAD_DIM), F32)
    for index, value in enumerate((dec[...], mem[...], target[...] // 256, target[...] % 256)):
        notes = jnp.where(row == index, wide(value), notes)
    notes = notes.astype(BF16)
    for head in range(q.shape[1] // HEAD_DIM):
        lanes = pl.ds(head * HEAD_DIM, HEAD_DIM)
        for part in range(parts):
            to = head * parts + part
            own = pl.ds(part * piece, piece)
            out_ref[to, pl.ds(0, mem_rows)] = k[:, lanes]
            out_ref[to, pl.ds(mem_rows, mem_rows)] = v[:, lanes]
            out_ref[to, pl.ds(at_q, piece)] = q[own, lanes]
            out_ref[to, pl.ds(at_q + piece, piece)] = r[own, lanes]
            out_ref[to, pl.ds(at_q + 2 * piece, note_rows)] = notes


def pack(q, r, k, v, dec, mem, target, parts):
    heads = q.shape[1] // HEAD_DIM
    depth = 2 * k.shape[0] + 2 * (q.shape[0] // parts) + 8
    arrays = (q, r, k, v, dec[None], mem[None], target[None])

    def kernel(*refs):
        pack_kernel(parts, *refs)

    return pl.pallas_call(
        kernel,
        in_specs=[pl.BlockSpec(memory_space=pltpu.HBM)] * len(arrays),
        out_specs=pl.BlockSpec(memory_space=pltpu.VMEM),
        out_shape=jax.ShapeDtypeStruct((heads * parts, depth, HEAD_DIM), BF16),
        scratch_shapes=[pltpu.VMEM(a.shape, a.dtype) for a in arrays]
        + [pltpu.SemaphoreType.DMA((len(arrays),))],
        compiler_params=pltpu.CompilerParams(vmem_limit_bytes=64 * MIB),
        name="pack",
    )(*arrays)


def attend_kernel(piece, q_ref, r_ref, k_ref, v_ref, dec_ref, mem_ref, out_ref):
    scores = lax.dot_general(
        q_ref[...], k_ref[...], (((1,), (1,)), ((), ())), preferred_element_type=F32
    )
    scores = scores * (1.0 / math.sqrt(HEAD_DIM))
    scores = jnp.where(dec_ref[...] == mem_ref[...], scores, -jnp.inf)
    top = jnp.max(scores, axis=1, keepdims=True)
    raised = jnp.exp(scores - top)
    weights = (raised / jnp.sum(raised, axis=1, keepdims=True)).astype(BF16)
    context = jnp.dot(weights, v_ref[...], preferred_element_type=F32).astype(BF16)
    summed = r_ref[...].astype(F32) + context.astype(F32)
    halves = out_ref.shape[0]
    summed = summed.reshape(-1, halves, piece // halves, HEAD_DIM)
    for half in range(halves):
        out_ref[half] = summed[:, half].reshape(-1, HEAD_DIM).astype(BF16)


def attend(q, r, k, v, dec, mem, piece, halves):
    rows, mem_rows = q.shape[0], k.shape[0]
    tile = 128
    whole = lambda i: (0, 0)
    step = lambda i: (i, 0)

    def kernel(*refs):
        attend_kernel(piece, *refs)

    return pl.pallas_call(
        kernel,
        grid=(rows // tile,),
        in_specs=[
            pl.BlockSpec((tile, HEAD_DIM), step),
            pl.BlockSpec((tile, HEAD_DIM), step),
            pl.BlockSpec((mem_rows, HEAD_DIM), whole),
            pl.BlockSpec((mem_rows, HEAD_DIM), whole),
            pl.BlockSpec((tile, 1), step),
            pl.BlockSpec((1, mem_rows), whole),
        ],
        out_specs=pl.BlockSpec((halves, tile // halves, HEAD_DIM), lambda i: (0, i, 0)),
        out_shape=jax.ShapeDtypeStruct((halves, rows // halves, HEAD_DIM), BF16),
        compiler_params=pltpu.CompilerParams(vmem_limit_bytes=24 * MIB),
        name="attend",
    )(q, r, k, v, dec, mem)


def head_kernel(vocab, info_ref, x_ref, gain_ref, bias_ref, t_ref, *rest):
    slabs = len(rest) - 7
    w_refs = rest[:slabs]
    out_ref, held, x_held, normed, logits, sems, x_sems = rest[slabs:]
    heads, sets, halves, rows, chunk = x_ref.shape
    x_copies = [
        pltpu.make_async_copy(x_ref.at[:, group], x_held.at[:, group], x_sems.at[group])
        for group in range(sets)
    ]
    copies = [
        pltpu.make_async_copy(w_refs[k], held.at[k], sems.at[k]) for k in range(slabs)
    ]
    for copy in x_copies + copies:
        copy.start()
    mine = info_ref[slabs]
    step = 16
    for group in range(sets):
        x_copies[group].wait()
        for low in range(0, rows, step):
            at = pl.ds(low, step)
            parts = [
                x_held[head, group, half, at].astype(F32)
                for half in range(halves)
                for head in range(heads)
            ]
            mean = jnp.sum(sum(parts[1:], parts[0]), axis=1, keepdims=True) * (1.0 / D)
            parts = [part - mean for part in parts]
            squares = [part * part for part in parts]
            var = jnp.sum(sum(squares[1:], squares[0]), axis=1, keepdims=True) * (1.0 / D)
            scale = lax.rsqrt(var + LN_EPS)
            for half in range(halves):
                base = jnp.where(mine == 0, half, 1 - half) * (heads * chunk)
                for head in range(heads):
                    lanes = pl.ds(pl.multiple_of(base + head * chunk, chunk), chunk)
                    value = parts[half * heads + head] * scale * gain_ref[:, lanes]
                    normed[pl.ds(group * rows + low, step), lanes] = (
                        value + bias_ref[:, lanes]
                    ).astype(BF16)
    total = sets * rows
    width = held.shape[2]
    for k in range(slabs):
        copies[k].wait()
        logits[:, pl.ds(k * width, width)] = jnp.dot(
            normed[...], held[k], preferred_element_type=F32
        )
    lane = lax.broadcasted_iota(jnp.int32, (step, 128), 1)
    for low in range(0, total, step):
        at = pl.ds(low, step)
        target = t_ref[at]
        top = logits[at, pl.ds(0, 128)]
        for col in range(128, slabs * width, 128):
            top = jnp.maximum(top, logits[at, pl.ds(col, 128)])
        top = jnp.max(top, axis=1, keepdims=True)
        exps = sums = picks = jnp.zeros((step, 128), F32)
        for k in range(slabs):
            offset = target - info_ref[k]
            for col in range(0, width, 128):
                part = logits[at, pl.ds(k * width + col, 128)]
                exps = exps + jnp.exp(part - top)
                sums = sums + part
                picks = picks + jnp.where(lane == offset - col, part, 0.0)
        lse = top + jnp.log(jnp.sum(exps, axis=1, keepdims=True))
        line = (1.0 - EPS_SMOOTH) * picks + (EPS_SMOOTH / vocab) * sums
        line = jnp.sum(line, axis=1, keepdims=True)
        pair = lax.broadcasted_iota(jnp.int32, (step, 2), 1)
        out_ref[at] = jnp.where(pair == 0, lse, line)


def head_stats(x, gain, bias, targets, slabs, info, vocab):
    heads, sets, halves, rows, chunk = x.shape
    total = sets * rows
    width = slabs[0].shape[1]

    def kernel(*refs):
        head_kernel(vocab, *refs)

    vmem = pl.BlockSpec(memory_space=pltpu.VMEM)
    hbm = pl.BlockSpec(memory_space=pltpu.HBM)
    return pl.pallas_call(
        kernel,
        in_specs=[pl.BlockSpec(memory_space=pltpu.SMEM), hbm, vmem, vmem, vmem]
        + [hbm] * len(slabs),
        out_specs=vmem,
        out_shape=jax.ShapeDtypeStruct((total, 2), F32),
        scratch_shapes=[
            pltpu.VMEM((len(slabs), D, width), BF16),
            pltpu.VMEM(x.shape, BF16),
            pltpu.VMEM((total, D), BF16),
            pltpu.VMEM((total, len(slabs) * width), F32),
            pltpu.SemaphoreType.DMA((len(slabs),)),
            pltpu.SemaphoreType.DMA((sets,)),
        ],
        compiler_params=pltpu.CompilerParams(vmem_limit_bytes=40 * MIB),
        name="head_stats",
    )(info, x, gain, bias, targets, *slabs)


def per_device(
    queries,
    residual,
    mem_keys,
    mem_values,
    dec_ids,
    mem_ids,
    targets,
    ln_gain,
    ln_bias,
    head_weight,
):
    enc, zh, zl, yhi = (lax.axis_index(name) for name in ("enc", "zh", "zl", "yhi"))
    enc_count, y_count = lax.axis_size("enc"), lax.axis_size("yhi")
    z = zh * lax.axis_size("zl") + zl
    z_count = lax.axis_size("zh") * lax.axis_size("zl")
    voc_count = z_count * y_count
    heads = queries.shape[1] // HEAD_DIM
    parts = voc_count // heads
    sets = parts // y_count
    rows, mem_rows = queries.shape[0], mem_keys.shape[0]
    piece = rows // parts
    slice_rows = piece // enc_count
    width = head_weight.shape[1]
    vocab = width * voc_count * enc_count

    with jax.named_scope("weights"):
        weight_y = lax.ppermute(head_weight, "yhi", SWAP)
        weight_e = lax.ppermute(head_weight, "enc", SWAP)
        weight_ye = lax.ppermute(head_weight, ("enc", "yhi"), CROSS)
    with jax.named_scope("pack"):
        message = pack(
            queries, residual, mem_keys, mem_values, dec_ids, mem_ids, targets, parts
        )
    with jax.named_scope("spread"):
        got = lax.all_to_all(message, VOC, 0, 0, tiled=True)
    with jax.named_scope("attention"):
        at_q = 2 * mem_rows
        take = lambda low, count: got[:, low : low + count].reshape(-1, HEAD_DIM)
        noted = got[:, at_q + 2 * piece : at_q + 2 * piece + 4].astype(jnp.int32)
        dec = lax.dynamic_slice_in_dim(
            noted[:, 0, :rows], (zl * y_count + yhi) * piece, piece, 1
        ).reshape(-1, 1)
        mem = noted[:, 1, :mem_rows].reshape(1, -1)
        target = noted[:, 2, :rows] * 256 + noted[:, 3, :rows]
        target = target.reshape(voc_count, sets, y_count * enc_count, slice_rows)
        target = lax.dynamic_index_in_dim(target, yhi * enc_count + enc, 2, False)
        target = target.transpose(1, 0, 2)
        halves = attend(
            take(at_q, piece),
            take(at_q + piece, piece),
            take(0, mem_rows),
            take(mem_rows, mem_rows),
            dec,
            mem,
            piece,
            enc_count,
        )
    early = int(voc_count * EARLY_SHARE)
    cut = early * slice_rows
    with jax.named_scope("halves"):
        kept = lax.dynamic_index_in_dim(halves, enc, 0, False)
        passed = lax.dynamic_index_in_dim(halves, 1 - enc, 0, False)
        handed = lax.ppermute(passed, "enc", SWAP)
        kept_beside = lax.ppermute(kept[cut:], "zl", SWAP)
        handed_beside = lax.ppermute(passed[cut:], ("enc", "zl"), CROSS)
        late_shard = jnp.stack(
            [jnp.stack([kept[cut:], handed[cut:]]), jnp.stack([kept_beside, handed_beside])]
        )
        early_shard = jnp.stack([kept[:cut], handed[:cut]])
    def head(full, target):
        with jax.named_scope("head"):
            stats = head_stats(
                full,
                ln_gain[None],
                ln_bias[None],
                target.reshape(-1, 1),
                (head_weight, weight_e, weight_y, weight_ye),
                info,
                vocab,
            )
            return stats.reshape(sets, -1, slice_rows, 2)

    with jax.named_scope("rows"):
        late_full = lax.all_gather(late_shard, "zh", axis=0)
        early_full = lax.all_gather(early_shard, ("zh", "zl"), axis=0)
        early_full = early_full.reshape((heads, sets) + early_full.shape[1:])
    slab = lambda e, y: ((e * voc_count) + z * y_count + y) * width
    info = jnp.stack(
        [
            slab(enc, yhi),
            slab(1 - enc, yhi),
            slab(enc, 1 - yhi),
            slab(1 - enc, 1 - yhi),
            enc,
        ]
    ).astype(jnp.int32)

    early_stats = head(early_full, target[:, :early])
    swapped = lambda a: jnp.where(zl == 0, a, a[::-1])
    late_stats = swapped(head(late_full, swapped(target[:, early:])))
    with jax.named_scope("merge"):
        stats = jnp.concatenate([early_stats, late_stats], axis=1).transpose(1, 3, 0, 2)
        stats = jnp.broadcast_to(
            stats.reshape(1, voc_count, 2, -1), (enc_count, voc_count, 2, sets * slice_rows)
        )
        merged = lax.all_to_all(
            stats.reshape(enc_count * voc_count, 2, -1), ("enc",) + VOC, 0, 0, tiled=True
        )
        merged = merged.reshape(enc_count, z_count, y_count, 2, sets, slice_rows)
        lse, line = merged[:, :, :, 0], merged[:, :, :, 1]
        top = jnp.max(lse, axis=1, keepdims=True)
        log_total = top[:, 0] + jnp.log(jnp.sum(jnp.exp(lse - top), axis=1))
        loss = log_total - jnp.sum(line, axis=1) + Z_COEF * log_total * log_total
        return loss.transpose(2, 1, 0, 3).reshape(rows)


def solution(mesh):
    shape = dict(mesh.shape)
    fine = Mesh(
        mesh.devices.reshape(shape["enc"], shape["blk"], shape["voc"] // 4, 2, 2),
        ("enc", "blk") + VOC,
    )
    held = ("blk",) + VOC
    in_specs = (
        P(held, "enc"),
        P(held, "enc"),
        P(held, "enc"),
        P(held, "enc"),
        P(held),
        P(held),
        P(held),
        P(),
        P(),
        P(None, ("enc",) + VOC),
    )
    return jax.shard_map(
        per_device, mesh=fine, in_specs=in_specs, out_specs=P(held), check_vma=False
    )
```

```python
import math

import jax
import jax.numpy as jnp
from jax import lax
from jax.experimental import pallas as pl
from jax.experimental.pallas import tpu as pltpu
from jax.sharding import Mesh
from jax.sharding import PartitionSpec as P

D = 2048
HEADS = 16
HEAD_DIM = D // HEADS

EPS_SMOOTH = 0.1
Z_COEF = 0.0001
LN_EPS = 1e-05

BF16 = jnp.bfloat16
F32 = jnp.float32
MIB = 1024 * 1024

Z = ("zq", "zr")
VOC = Z + ("yhi",)
SWAP = [(0, 1), (1, 0)]


def pack_kernel(parts, *refs):
    sources, out_ref, (q, r, k, v, dec, mem, target), sems = (
        refs[:7],
        refs[7],
        refs[8:15],
        refs[15],
    )
    held = (q, r, k, v, dec, mem, target)
    copies = [
        pltpu.make_async_copy(source, buffer, sems.at[index])
        for index, (source, buffer) in enumerate(zip(sources, held))
    ]
    for copy in copies:
        copy.start()
    for copy in copies:
        copy.wait()
    mem_rows = k.shape[0]
    rows = q.shape[0]
    piece = rows // parts
    at_q = 2 * mem_rows
    note_rows = out_ref.shape[1] - at_q - 2 * piece
    wide = lambda a: jnp.pad(a.astype(F32), ((0, 0), (0, HEAD_DIM - a.shape[1])))
    row = lax.broadcasted_iota(jnp.int32, (note_rows, HEAD_DIM), 0)
    notes = jnp.zeros((note_rows, HEAD_DIM), F32)
    for index, value in enumerate((dec[...], mem[...], target[...] // 256, target[...] % 256)):
        notes = jnp.where(row == index, wide(value), notes)
    notes = notes.astype(BF16)
    for head in range(q.shape[1] // HEAD_DIM):
        lanes = pl.ds(head * HEAD_DIM, HEAD_DIM)
        for part in range(parts):
            to = head * parts + part
            own = pl.ds(part * piece, piece)
            out_ref[to, pl.ds(0, mem_rows)] = k[:, lanes]
            out_ref[to, pl.ds(mem_rows, mem_rows)] = v[:, lanes]
            out_ref[to, pl.ds(at_q, piece)] = q[own, lanes]
            out_ref[to, pl.ds(at_q + piece, piece)] = r[own, lanes]
            out_ref[to, pl.ds(at_q + 2 * piece, note_rows)] = notes


def pack(q, r, k, v, dec, mem, target, parts):
    heads = q.shape[1] // HEAD_DIM
    depth = 2 * k.shape[0] + 2 * (q.shape[0] // parts) + 8
    arrays = (q, r, k, v, dec[None], mem[None], target[None])

    def kernel(*refs):
        pack_kernel(parts, *refs)

    return pl.pallas_call(
        kernel,
        in_specs=[pl.BlockSpec(memory_space=pltpu.HBM)] * len(arrays),
        out_specs=pl.BlockSpec(memory_space=pltpu.VMEM),
        out_shape=jax.ShapeDtypeStruct((heads * parts, depth, HEAD_DIM), BF16),
        scratch_shapes=[pltpu.VMEM(a.shape, a.dtype) for a in arrays]
        + [pltpu.SemaphoreType.DMA((len(arrays),))],
        compiler_params=pltpu.CompilerParams(vmem_limit_bytes=64 * MIB),
        name="pack",
    )(*arrays)


def attend_kernel(piece, q_ref, r_ref, k_ref, v_ref, dec_ref, mem_ref, out_ref):
    scores = lax.dot_general(
        q_ref[...], k_ref[...], (((1,), (1,)), ((), ())), preferred_element_type=F32
    )
    scores = scores * (1.0 / math.sqrt(HEAD_DIM))
    scores = jnp.where(dec_ref[...] == mem_ref[...], scores, -jnp.inf)
    top = jnp.max(scores, axis=1, keepdims=True)
    raised = jnp.exp(scores - top)
    weights = (raised / jnp.sum(raised, axis=1, keepdims=True)).astype(BF16)
    context = jnp.dot(weights, v_ref[...], preferred_element_type=F32).astype(BF16)
    summed = r_ref[...].astype(F32) + context.astype(F32)
    halves = out_ref.shape[0]
    summed = summed.reshape(-1, halves, piece // halves, HEAD_DIM)
    for half in range(halves):
        out_ref[half] = summed[:, half].reshape(-1, HEAD_DIM).astype(BF16)


def attend(q, r, k, v, dec, mem, piece, halves):
    rows, mem_rows = q.shape[0], k.shape[0]
    tile = 128
    whole = lambda i: (0, 0)
    step = lambda i: (i, 0)

    def kernel(*refs):
        attend_kernel(piece, *refs)

    return pl.pallas_call(
        kernel,
        grid=(rows // tile,),
        in_specs=[
            pl.BlockSpec((tile, HEAD_DIM), step),
            pl.BlockSpec((tile, HEAD_DIM), step),
            pl.BlockSpec((mem_rows, HEAD_DIM), whole),
            pl.BlockSpec((mem_rows, HEAD_DIM), whole),
            pl.BlockSpec((tile, 1), step),
            pl.BlockSpec((1, mem_rows), whole),
        ],
        out_specs=pl.BlockSpec((halves, tile // halves, HEAD_DIM), lambda i: (0, i, 0)),
        out_shape=jax.ShapeDtypeStruct((halves, rows // halves, HEAD_DIM), BF16),
        compiler_params=pltpu.CompilerParams(vmem_limit_bytes=24 * MIB),
        name="attend",
    )(q, r, k, v, dec, mem)


def head_kernel(vocab, slabs, places, sets, info_ref, gain_ref, bias_ref, t_ref, *rest):
    out_ref, held, normed, logits, columns, turned, sems = rest[-7:]
    x_refs, w_refs = rest[: -7 - slabs], rest[-7 - slabs : -7]
    turns = 1 + max(place[2] for place in places)
    copies = [
        pltpu.make_async_copy(w_refs[k], held.at[k], sems.at[k]) for k in range(slabs)
    ]
    for copy in copies:
        copy.start()
    enc, z, own_rows = (info_ref[slabs + index] for index in range(3))
    halves, rows, chunk = x_refs[0].shape[1:]
    heads = len(places) // sets
    total = sets * rows
    width = held.shape[2]
    side = columns.shape[1]
    step = 16
    lane = lax.broadcasted_iota(jnp.int32, (step, side), 1)

    voc_count = t_ref.shape[0]
    share = rows // voc_count
    filler = jnp.zeros((side - voc_count, side), F32)
    turned[...] = jnp.transpose(jnp.concatenate([t_ref[...], filler], axis=0))
    orders = [lax.rem(z + group, sets) for group in range(sets)]
    for group in range(sets):
        at = pl.multiple_of(orders[group] * (side // 2 // sets) + own_rows, share)
        block = turned[pl.ds(at, share)]
        for voc in range(voc_count):
            columns[pl.ds(group * rows + voc * share, share)] = jnp.broadcast_to(
                block[:, voc : voc + 1], (share, side)
            )

    for group in range(sets):
        order = [
            (place, half)
            for place in places
            if place[2] % sets == group
            for half in range(halves)
        ]
        bases = []
        for (_, _, turn, index), half in order:
            head = index * (turns // sets) + lax.rem(z + turn, turns) // sets
            at_half = jnp.where(enc == 0, half, 1 - half)
            bases.append(pl.multiple_of((at_half * heads + head) * chunk, chunk))
        for low in range(0, rows, step):
            at = pl.ds(low, step)
            parts = [
                x_refs[place[0]][place[1], half, at].astype(F32) for place, half in order
            ]
            mean = jnp.sum(sum(parts[1:], parts[0]), axis=1, keepdims=True) * (1.0 / D)
            parts = [part - mean for part in parts]
            squares = [part * part for part in parts]
            var = jnp.sum(sum(squares[1:], squares[0]), axis=1, keepdims=True) * (1.0 / D)
            scale = lax.rsqrt(var + LN_EPS)
            for base, part in zip(bases, parts):
                lanes = pl.ds(base, chunk)
                value = part * scale * gain_ref[:, lanes] + bias_ref[:, lanes]
                normed[pl.ds(group * rows + low, step), lanes] = value.astype(BF16)

    for k in range(slabs):
        copies[k].wait()
        logits[:, pl.ds(k * width, width)] = jnp.dot(
            normed[...], held[k], preferred_element_type=F32
        )

    for low in range(0, total, step):
        at = pl.ds(low, step)
        target = columns[at].astype(jnp.int32)
        top = logits[at, pl.ds(0, side)]
        for col in range(side, slabs * width, side):
            top = jnp.maximum(top, logits[at, pl.ds(col, side)])
        top = jnp.max(top, axis=1, keepdims=True)
        exps = sums = picks = jnp.zeros((step, side), F32)
        for k in range(slabs):
            offset = target - info_ref[k] - lane
            for col in range(0, width, side):
                part = logits[at, pl.ds(k * width + col, side)]
                exps = exps + jnp.exp(part - top)
                sums = sums + part
                picks = picks + jnp.where(offset == col, part, 0.0)
        lse = top + jnp.log(jnp.sum(exps, axis=1, keepdims=True))
        line = (1.0 - EPS_SMOOTH) * picks + (EPS_SMOOTH / vocab) * sums
        line = jnp.sum(line, axis=1, keepdims=True)
        columns[at] = jnp.where(lane == 0, lse, line)

    for group in range(sets):
        for low in range(0, rows, side):
            block = jnp.transpose(columns[pl.ds(group * rows + low, side)])
            lanes = pl.ds(pl.multiple_of(orders[group] * rows + low, side), side)
            out_ref[:, lanes] = block[: out_ref.shape[0]]


def head_stats(xs, places, sets, gain, bias, targets, slabs, info, vocab):
    total = sets * xs[0].shape[2]
    width = slabs[0].shape[1]

    def kernel(*refs):
        head_kernel(vocab, len(slabs), places, sets, *refs)

    vmem = pl.BlockSpec(memory_space=pltpu.VMEM)
    hbm = pl.BlockSpec(memory_space=pltpu.HBM)
    stats = pl.pallas_call(
        kernel,
        in_specs=[pl.BlockSpec(memory_space=pltpu.SMEM), vmem, vmem, vmem]
        + [vmem] * len(xs)
        + [hbm] * len(slabs),
        out_specs=vmem,
        out_shape=jax.ShapeDtypeStruct((8, total), F32),
        scratch_shapes=[
            pltpu.VMEM((len(slabs), D, width), BF16),
            pltpu.VMEM((total, D), BF16),
            pltpu.VMEM((total, len(slabs) * width), F32),
            pltpu.VMEM((total, 128), F32),
            pltpu.VMEM((128, 128), F32),
            pltpu.SemaphoreType.DMA((len(slabs),)),
        ],
        compiler_params=pltpu.CompilerParams(vmem_limit_bytes=40 * MIB),
        name="head_stats",
    )(info, gain, bias, targets, *xs, *slabs)
    return stats[:2]


def per_device(
    queries,
    residual,
    mem_keys,
    mem_values,
    dec_ids,
    mem_ids,
    targets,
    ln_gain,
    ln_bias,
    head_weight,
):
    enc, z, yhi = (lax.axis_index(name) for name in ("enc", Z, "yhi"))
    enc_count, z_count, y_count = (lax.axis_size(name) for name in ("enc", Z, "yhi"))
    voc_count = z_count * y_count
    heads = queries.shape[1] // HEAD_DIM
    parts = voc_count // heads
    sets = parts // y_count
    rows, mem_rows = queries.shape[0], mem_keys.shape[0]
    piece = rows // parts
    slice_rows = piece // enc_count
    width = head_weight.shape[1]
    vocab = width * voc_count * enc_count

    with jax.named_scope("weights"):
        weight_y = lax.ppermute(head_weight, "yhi", SWAP)
        weight_e = lax.ppermute(head_weight, "enc", SWAP)
    with jax.named_scope("pack"):
        message = pack(
            queries, residual, mem_keys, mem_values, dec_ids, mem_ids, targets, parts
        )
    with jax.named_scope("spread"):
        got = lax.all_to_all(message, VOC, 0, 0, tiled=True)
        got, weight_e = lax.optimization_barrier((got, weight_e))
    with jax.named_scope("attention"):
        at_q = 2 * mem_rows
        take = lambda low, count: got[:, low : low + count].reshape(-1, HEAD_DIM)
        noted = got[:, at_q + 2 * piece : at_q + 2 * piece + 4].astype(jnp.int32)
        dec = lax.dynamic_slice_in_dim(
            noted[:, 0, :rows], (z % sets * y_count + yhi) * piece, piece, 1
        ).reshape(-1, 1)
        mem = noted[:, 1, :mem_rows].reshape(1, -1)
        target = (noted[:, 2] * 256 + noted[:, 3]).astype(F32)
        halves = attend(
            take(at_q, piece),
            take(at_q + piece, piece),
            take(0, mem_rows),
            take(mem_rows, mem_rows),
            dec,
            mem,
            piece,
            enc_count,
        )
    with jax.named_scope("halves"):
        kept = lax.dynamic_index_in_dim(halves, enc, 0, False)
        passed = lax.dynamic_index_in_dim(halves, 1 - enc, 0, False)
        shard = jnp.stack([kept, lax.ppermute(passed, "enc", SWAP)])
    with jax.named_scope("rows"):
        up = [(i, (i + 1) % z_count) for i in range(z_count)]
        down = [(i, (i - 1) % z_count) for i in range(z_count)]
        fours = lax.all_gather(shard, "zq", axis=0)
        fours, weight_y = lax.optimization_barrier((fours, weight_y))
        below, above = lax.ppermute(fours, Z, up), lax.ppermute(fours, Z, down)
        cut = fours.shape[0] // 2
        opposite = lax.ppermute(below[:cut], Z, up), lax.ppermute(above[cut:], Z, down)
        bundles = [fours, above, opposite[0], opposite[1], below]
        places = [
            (ref, index - first, turn, index)
            for turn, ref, first, last in (
                (0, 0, 0, 2 * cut),
                (1, 1, 0, 2 * cut),
                (2, 2, 0, cut),
                (2, 3, cut, 2 * cut),
                (3, 4, 0, 2 * cut),
            )
            for index in range(first, last)
        ]
    with jax.named_scope("weights"):
        weight_ye = lax.ppermute(weight_y, "enc", SWAP)
    with jax.named_scope("head"):
        slab = lambda e, y: ((e * voc_count) + z * y_count + y) * width
        info = jnp.stack(
            [
                slab(enc, yhi),
                slab(1 - enc, yhi),
                slab(enc, 1 - yhi),
                slab(1 - enc, 1 - yhi),
                enc,
                z,
                yhi * piece + enc * slice_rows,
            ]
        ).astype(jnp.int32)
        stats = head_stats(
            bundles,
            places,
            sets,
            ln_gain[None],
            ln_bias[None],
            target,
            (head_weight, weight_e, weight_y, weight_ye),
            info,
            vocab,
        )
        stats = stats.reshape(2, sets, voc_count, slice_rows)
    with jax.named_scope("merge"):
        stats = stats.transpose(2, 0, 1, 3)
        stats = jnp.broadcast_to(
            stats.reshape(1, voc_count, 2, -1), (enc_count, voc_count, 2, sets * slice_rows)
        )
        merged = lax.all_to_all(
            stats.reshape(enc_count * voc_count, 2, -1), ("enc",) + VOC, 0, 0, tiled=True
        )
        merged = merged.reshape(enc_count, z_count, y_count, 2, sets, slice_rows)
        lse, line = merged[:, :, :, 0], merged[:, :, :, 1]
        top = jnp.max(lse, axis=1, keepdims=True)
        log_total = top[:, 0] + jnp.log(jnp.sum(jnp.exp(lse - top), axis=1))
        loss = log_total - jnp.sum(line, axis=1) + Z_COEF * log_total * log_total
        return loss.transpose(2, 1, 0, 3).reshape(rows)


def solution(mesh):
    shape = dict(mesh.shape)
    fine = Mesh(
        mesh.devices.reshape(shape["enc"], shape["blk"], shape["voc"] // 8, 4, 2),
        ("enc", "blk") + VOC,
    )
    held = ("blk",) + VOC
    in_specs = (
        P(held, "enc"),
        P(held, "enc"),
        P(held, "enc"),
        P(held, "enc"),
        P(held),
        P(held),
        P(held),
        P(),
        P(),
        P(None, ("enc",) + VOC),
    )
    return jax.shard_map(
        per_device, mesh=fine, in_specs=in_specs, out_specs=P(held), check_vma=False
    )
```

```python
import math

import jax
import jax.numpy as jnp
from jax import lax
from jax.experimental import pallas as pl
from jax.experimental.pallas import tpu as pltpu
from jax.sharding import Mesh
from jax.sharding import PartitionSpec as P

D = 2048
HEADS = 16
HEAD_DIM = D // HEADS

EPS_SMOOTH = 0.1
Z_COEF = 0.0001
LN_EPS = 1e-05

BF16 = jnp.bfloat16
F32 = jnp.float32
MIB = 1024 * 1024

Z = ("zq", "zr")
VOC = Z + ("yhi",)
SWAP = [(0, 1), (1, 0)]


def pack_kernel(parts, *refs):
    sources, out_ref, (q, r, k, v, dec, mem, target), sems = (
        refs[:7],
        refs[7],
        refs[8:15],
        refs[15],
    )
    held = (q, r, k, v, dec, mem, target)
    copies = [
        pltpu.make_async_copy(source, buffer, sems.at[index])
        for index, (source, buffer) in enumerate(zip(sources, held))
    ]
    for copy in copies:
        copy.start()
    for copy in copies:
        copy.wait()
    mem_rows = k.shape[0]
    rows = q.shape[0]
    piece = rows // parts
    at_q = 2 * mem_rows
    note_rows = out_ref.shape[1] - at_q - 2 * piece
    wide = lambda a: jnp.pad(a.astype(F32), ((0, 0), (0, HEAD_DIM - a.shape[1])))
    row = lax.broadcasted_iota(jnp.int32, (note_rows, HEAD_DIM), 0)
    notes = jnp.zeros((note_rows, HEAD_DIM), F32)
    for index, value in enumerate((dec[...], mem[...], target[...] // 256, target[...] % 256)):
        notes = jnp.where(row == index, wide(value), notes)
    notes = notes.astype(BF16)
    for head in range(q.shape[1] // HEAD_DIM):
        lanes = pl.ds(head * HEAD_DIM, HEAD_DIM)
        for part in range(parts):
            to = head * parts + part
            own = pl.ds(part * piece, piece)
            out_ref[to, pl.ds(0, mem_rows)] = k[:, lanes]
            out_ref[to, pl.ds(mem_rows, mem_rows)] = v[:, lanes]
            out_ref[to, pl.ds(at_q, piece)] = q[own, lanes]
            out_ref[to, pl.ds(at_q + piece, piece)] = r[own, lanes]
            out_ref[to, pl.ds(at_q + 2 * piece, note_rows)] = notes


def pack(q, r, k, v, dec, mem, target, parts):
    heads = q.shape[1] // HEAD_DIM
    depth = 2 * k.shape[0] + 2 * (q.shape[0] // parts) + 8
    arrays = (q, r, k, v, dec[None], mem[None], target[None])

    def kernel(*refs):
        pack_kernel(parts, *refs)

    return pl.pallas_call(
        kernel,
        in_specs=[pl.BlockSpec(memory_space=pltpu.HBM)] * len(arrays),
        out_specs=pl.BlockSpec(memory_space=pltpu.VMEM),
        out_shape=jax.ShapeDtypeStruct((heads * parts, depth, HEAD_DIM), BF16),
        scratch_shapes=[pltpu.VMEM(a.shape, a.dtype) for a in arrays]
        + [pltpu.SemaphoreType.DMA((len(arrays),))],
        compiler_params=pltpu.CompilerParams(vmem_limit_bytes=64 * MIB),
        name="pack",
    )(*arrays)


def attend_kernel(piece, q_ref, r_ref, k_ref, v_ref, dec_ref, mem_ref, out_ref):
    scores = lax.dot_general(
        q_ref[...], k_ref[...], (((1,), (1,)), ((), ())), preferred_element_type=F32
    )
    scores = scores * (1.0 / math.sqrt(HEAD_DIM))
    scores = jnp.where(dec_ref[...] == mem_ref[...], scores, -jnp.inf)
    top = jnp.max(scores, axis=1, keepdims=True)
    raised = jnp.exp(scores - top)
    weights = (raised / jnp.sum(raised, axis=1, keepdims=True)).astype(BF16)
    context = jnp.dot(weights, v_ref[...], preferred_element_type=F32).astype(BF16)
    summed = r_ref[...].astype(F32) + context.astype(F32)
    halves = out_ref.shape[0]
    summed = summed.reshape(-1, halves, piece // halves, HEAD_DIM)
    for half in range(halves):
        out_ref[half] = summed[:, half].reshape(-1, HEAD_DIM).astype(BF16)


def attend(q, r, k, v, dec, mem, piece, halves):
    rows, mem_rows = q.shape[0], k.shape[0]
    tile = 128
    whole = lambda i: (0, 0)
    step = lambda i: (i, 0)

    def kernel(*refs):
        attend_kernel(piece, *refs)

    return pl.pallas_call(
        kernel,
        grid=(rows // tile,),
        in_specs=[
            pl.BlockSpec((tile, HEAD_DIM), step),
            pl.BlockSpec((tile, HEAD_DIM), step),
            pl.BlockSpec((mem_rows, HEAD_DIM), whole),
            pl.BlockSpec((mem_rows, HEAD_DIM), whole),
            pl.BlockSpec((tile, 1), step),
            pl.BlockSpec((1, mem_rows), whole),
        ],
        out_specs=pl.BlockSpec((halves, tile // halves, HEAD_DIM), lambda i: (0, i, 0)),
        out_shape=jax.ShapeDtypeStruct((halves, rows // halves, HEAD_DIM), BF16),
        compiler_params=pltpu.CompilerParams(vmem_limit_bytes=24 * MIB),
        name="attend",
    )(q, r, k, v, dec, mem)


def head_kernel(
    vocab, slabs, places, group, sets, info_ref, gain_ref, bias_ref, t_ref, *rest
):
    out_ref, held, normed, logits, columns, turned, sems = rest[-7:]
    x_refs, w_refs = rest[: -7 - slabs], rest[-7 - slabs : -7]
    copies = [
        pltpu.make_async_copy(w_refs[k], held.at[k], sems.at[k]) for k in range(slabs)
    ]
    for copy in copies:
        copy.start()
    turns = 4
    enc, z, own_rows = (info_ref[slabs + index] for index in range(3))
    halves, rows, chunk = x_refs[0].shape[1:]
    heads = len(places)
    width = w_refs[0].shape[1]
    side = columns.shape[1]
    step = 16
    lane = lax.broadcasted_iota(jnp.int32, (step, side), 1)

    voc_count = t_ref.shape[0]
    share = rows // voc_count
    filler = jnp.zeros((side - voc_count, side), F32)
    turned[...] = jnp.transpose(jnp.concatenate([t_ref[...], filler], axis=0))
    at = pl.multiple_of(lax.rem(z + group, sets) * (side // 2 // sets) + own_rows, share)
    block = turned[pl.ds(at, share)]
    for voc in range(voc_count):
        columns[pl.ds(voc * share, share)] = jnp.broadcast_to(
            block[:, voc : voc + 1], (share, side)
        )

    order = [(place, half) for place in places for half in range(halves)]
    bases = []
    for (_, _, turn, index), half in order:
        head = index * (turns // sets) + lax.rem(z + turn, turns) // sets
        at_half = jnp.where(enc == 0, half, 1 - half)
        bases.append(pl.multiple_of((at_half * heads + head) * chunk, chunk))
    for low in range(0, rows, step):
        at = pl.ds(low, step)
        parts = [x_refs[place[0]][place[1], half, at].astype(F32) for place, half in order]
        mean = jnp.sum(sum(parts[1:], parts[0]), axis=1, keepdims=True) * (1.0 / D)
        parts = [part - mean for part in parts]
        squares = [part * part for part in parts]
        var = jnp.sum(sum(squares[1:], squares[0]), axis=1, keepdims=True) * (1.0 / D)
        scale = lax.rsqrt(var + LN_EPS)
        for base, part in zip(bases, parts):
            lanes = pl.ds(base, chunk)
            value = part * scale * gain_ref[:, lanes] + bias_ref[:, lanes]
            normed[at, lanes] = value.astype(BF16)

    for k in range(slabs):
        copies[k].wait()
        logits[:, pl.ds(k * width, width)] = jnp.dot(
            normed[...], held[k], preferred_element_type=F32
        )

    for low in range(0, rows, step):
        at = pl.ds(low, step)
        target = columns[at].astype(jnp.int32)
        top = logits[at, pl.ds(0, side)]
        for col in range(side, slabs * width, side):
            top = jnp.maximum(top, logits[at, pl.ds(col, side)])
        top = jnp.max(top, axis=1, keepdims=True)
        exps = sums = picks = jnp.zeros((step, side), F32)
        for k in range(slabs):
            offset = target - info_ref[k] - lane
            for col in range(0, width, side):
                part = logits[at, pl.ds(k * width + col, side)]
                exps = exps + jnp.exp(part - top)
                sums = sums + part
                picks = picks + jnp.where(offset == col, part, 0.0)
        lse = top + jnp.log(jnp.sum(exps, axis=1, keepdims=True))
        line = (1.0 - EPS_SMOOTH) * picks + (EPS_SMOOTH / vocab) * sums
        line = jnp.sum(line, axis=1, keepdims=True)
        columns[at] = jnp.where(lane == 0, lse, line)

    for low in range(0, rows, side):
        block = jnp.transpose(columns[pl.ds(low, side)])
        out_ref[:, pl.ds(low, side)] = block[: out_ref.shape[0]]


def head_stats(xs, places, group, sets, gain, bias, targets, slabs, info, vocab):
    rows = xs[0].shape[2]
    width = slabs[0].shape[1]

    def kernel(*refs):
        head_kernel(vocab, len(slabs), places, group, sets, *refs)

    vmem = pl.BlockSpec(memory_space=pltpu.VMEM)
    hbm = pl.BlockSpec(memory_space=pltpu.HBM)
    stats = pl.pallas_call(
        kernel,
        in_specs=[pl.BlockSpec(memory_space=pltpu.SMEM)]
        + [vmem] * (3 + len(xs))
        + [hbm] * len(slabs),
        out_specs=vmem,
        out_shape=jax.ShapeDtypeStruct((8, rows), F32),
        scratch_shapes=[
            pltpu.VMEM((len(slabs), D, width), BF16),
            pltpu.VMEM((rows, D), BF16),
            pltpu.VMEM((rows, len(slabs) * width), F32),
            pltpu.VMEM((rows, 128), F32),
            pltpu.VMEM((128, 128), F32),
            pltpu.SemaphoreType.DMA((len(slabs),)),
        ],
        compiler_params=pltpu.CompilerParams(vmem_limit_bytes=32 * MIB),
        cost_estimate=pl.CostEstimate(
            flops=2 * rows * D * len(slabs) * width,
            bytes_accessed=2 * D * len(slabs) * width,
            transcendentals=rows * len(slabs) * width,
        ),
        name="head_stats",
    )(info, gain, bias, targets, *xs, *slabs)
    return stats[:2]


def per_device(
    queries,
    residual,
    mem_keys,
    mem_values,
    dec_ids,
    mem_ids,
    targets,
    ln_gain,
    ln_bias,
    head_weight,
):
    enc, z, yhi = (lax.axis_index(name) for name in ("enc", Z, "yhi"))
    enc_count, z_count, y_count = (lax.axis_size(name) for name in ("enc", Z, "yhi"))
    voc_count = z_count * y_count
    heads = queries.shape[1] // HEAD_DIM
    parts = voc_count // heads
    sets = parts // y_count
    rows, mem_rows = queries.shape[0], mem_keys.shape[0]
    piece = rows // parts
    slice_rows = piece // enc_count
    width = head_weight.shape[1]
    vocab = width * voc_count * enc_count

    with jax.named_scope("weights"):
        weight_y = lax.ppermute(head_weight, "yhi", SWAP)
        weight_e = lax.ppermute(head_weight, "enc", SWAP)
    with jax.named_scope("pack"):
        message = pack(
            queries, residual, mem_keys, mem_values, dec_ids, mem_ids, targets, parts
        )
    with jax.named_scope("spread"):
        got = lax.all_to_all(message, VOC, 0, 0, tiled=True)
        got, weight_e = lax.optimization_barrier((got, weight_e))
    with jax.named_scope("attention"):
        at_q = 2 * mem_rows
        take = lambda low, count: got[:, low : low + count].reshape(-1, HEAD_DIM)
        noted = got[:, at_q + 2 * piece : at_q + 2 * piece + 4].astype(jnp.int32)
        dec = lax.dynamic_slice_in_dim(
            noted[:, 0, :rows], (z % sets * y_count + yhi) * piece, piece, 1
        ).reshape(-1, 1)
        mem = noted[:, 1, :mem_rows].reshape(1, -1)
        target = (noted[:, 2] * 256 + noted[:, 3]).astype(F32)
        halves = attend(
            take(at_q, piece),
            take(at_q + piece, piece),
            take(0, mem_rows),
            take(mem_rows, mem_rows),
            dec,
            mem,
            piece,
            enc_count,
        )
    with jax.named_scope("halves"):
        kept = lax.dynamic_index_in_dim(halves, enc, 0, False)
        passed = lax.dynamic_index_in_dim(halves, 1 - enc, 0, False)
        shard = jnp.stack([kept, lax.ppermute(passed, "enc", SWAP)])
    with jax.named_scope("rows"):
        up = [(i, (i + 1) % z_count) for i in range(z_count)]
        down = [(i, (i - 1) % z_count) for i in range(z_count)]
        fours = lax.all_gather(shard, "zq", axis=0)
        fours, weight_y = lax.optimization_barrier((fours, weight_y))
        cut = fours.shape[0] // 2
        low, high = fours[:cut], fours[cut:]
        below_low, above_high = lax.ppermute(low, Z, up), lax.ppermute(high, Z, down)
        below_high, above_low = lax.ppermute(high, Z, up), lax.ppermute(low, Z, down)
        far_low, far_high = lax.ppermute(below_low, Z, up), lax.ppermute(above_high, Z, down)
    with jax.named_scope("weights"):
        weight_ye = lax.ppermute(weight_y, "enc", SWAP)
    with jax.named_scope("head"):
        slab = lambda e, y: ((e * voc_count) + z * y_count + y) * width
        info = jnp.stack(
            [
                slab(enc, yhi),
                slab(1 - enc, yhi),
                slab(enc, 1 - yhi),
                slab(1 - enc, 1 - yhi),
                enc,
                z,
                yhi * piece + enc * slice_rows,
            ]
        ).astype(jnp.int32)
        halved = lambda ref, turn, first: [
            (ref, index, turn, first + index) for index in range(cut)
        ]

        def head(group, xs, places):
            found = head_stats(
                xs,
                places,
                group,
                sets,
                ln_gain[None],
                ln_bias[None],
                target,
                (head_weight, weight_e, weight_y, weight_ye),
                info,
                vocab,
            )
            return found.reshape(2, 1, voc_count, slice_rows)

        other = head(
            1,
            [above_low, above_high, below_low, below_high],
            halved(0, 1, 0) + halved(1, 1, cut) + halved(2, 3, 0) + halved(3, 3, cut),
        )
        same = head(
            0,
            [fours, far_low, far_high],
            [(0, index, 0, index) for index in range(2 * cut)]
            + halved(1, 2, 0)
            + halved(2, 2, cut),
        )
        stats = jnp.where(
            z % sets == 0,
            jnp.concatenate([same, other], axis=1),
            jnp.concatenate([other, same], axis=1),
        )
    with jax.named_scope("merge"):
        stats = stats.transpose(2, 0, 1, 3)
        stats = jnp.broadcast_to(
            stats.reshape(1, voc_count, 2, -1), (enc_count, voc_count, 2, sets * slice_rows)
        )
        merged = lax.all_to_all(
            stats.reshape(enc_count * voc_count, 2, -1), ("enc",) + VOC, 0, 0, tiled=True
        )
        merged = merged.reshape(enc_count, z_count, y_count, 2, sets, slice_rows)
        lse, line = merged[:, :, :, 0], merged[:, :, :, 1]
        top = jnp.max(lse, axis=1, keepdims=True)
        log_total = top[:, 0] + jnp.log(jnp.sum(jnp.exp(lse - top), axis=1))
        loss = log_total - jnp.sum(line, axis=1) + Z_COEF * log_total * log_total
        return loss.transpose(2, 1, 0, 3).reshape(rows)


def solution(mesh):
    shape = dict(mesh.shape)
    fine = Mesh(
        mesh.devices.reshape(shape["enc"], shape["blk"], shape["voc"] // 8, 4, 2),
        ("enc", "blk") + VOC,
    )
    held = ("blk",) + VOC
    in_specs = (
        P(held, "enc"),
        P(held, "enc"),
        P(held, "enc"),
        P(held, "enc"),
        P(held),
        P(held),
        P(held),
        P(),
        P(),
        P(None, ("enc",) + VOC),
    )
    return jax.shard_map(
        per_device, mesh=fine, in_specs=in_specs, out_specs=P(held), check_vma=False
    )
```

```python
import math

import jax
import jax.numpy as jnp
from jax import lax
from jax.experimental import pallas as pl
from jax.experimental.pallas import tpu as pltpu
from jax.sharding import Mesh
from jax.sharding import PartitionSpec as P

D = 2048
HEADS = 16
HEAD_DIM = D // HEADS

EPS_SMOOTH = 0.1
Z_COEF = 0.0001
LN_EPS = 1e-05

BF16 = jnp.bfloat16
F32 = jnp.float32
MIB = 1024 * 1024

Z = ("zq", "zr")
VOC = Z + ("yhi",)
SWAP = [(0, 1), (1, 0)]


def pack_kernel(parts, *refs):
    sources, out_ref, (q, r, k, v, dec, mem, target), sems = (
        refs[:7],
        refs[7],
        refs[8:15],
        refs[15],
    )
    held = (q, r, k, v, dec, mem, target)
    copies = [
        pltpu.make_async_copy(source, buffer, sems.at[index])
        for index, (source, buffer) in enumerate(zip(sources, held))
    ]
    for copy in copies:
        copy.start()
    for copy in copies:
        copy.wait()
    mem_rows = k.shape[0]
    rows = q.shape[0]
    piece = rows // parts
    at_q = 2 * mem_rows
    note_rows = out_ref.shape[1] - at_q - 2 * piece
    wide = lambda a: jnp.pad(a.astype(F32), ((0, 0), (0, HEAD_DIM - a.shape[1])))
    row = lax.broadcasted_iota(jnp.int32, (note_rows, HEAD_DIM), 0)
    notes = jnp.zeros((note_rows, HEAD_DIM), F32)
    for index, value in enumerate((dec[...], mem[...], target[...] // 256, target[...] % 256)):
        notes = jnp.where(row == index, wide(value), notes)
    notes = notes.astype(BF16)
    for head in range(q.shape[1] // HEAD_DIM):
        lanes = pl.ds(head * HEAD_DIM, HEAD_DIM)
        for part in range(parts):
            to = head * parts + part
            own = pl.ds(part * piece, piece)
            out_ref[to, pl.ds(0, mem_rows)] = k[:, lanes]
            out_ref[to, pl.ds(mem_rows, mem_rows)] = v[:, lanes]
            out_ref[to, pl.ds(at_q, piece)] = q[own, lanes]
            out_ref[to, pl.ds(at_q + piece, piece)] = r[own, lanes]
            out_ref[to, pl.ds(at_q + 2 * piece, note_rows)] = notes


def pack(q, r, k, v, dec, mem, target, parts):
    heads = q.shape[1] // HEAD_DIM
    depth = 2 * k.shape[0] + 2 * (q.shape[0] // parts) + 8
    arrays = (q, r, k, v, dec[None], mem[None], target[None])

    def kernel(*refs):
        pack_kernel(parts, *refs)

    return pl.pallas_call(
        kernel,
        in_specs=[pl.BlockSpec(memory_space=pltpu.HBM)] * len(arrays),
        out_specs=pl.BlockSpec(memory_space=pltpu.VMEM),
        out_shape=jax.ShapeDtypeStruct((heads * parts, depth, HEAD_DIM), BF16),
        scratch_shapes=[pltpu.VMEM(a.shape, a.dtype) for a in arrays]
        + [pltpu.SemaphoreType.DMA((len(arrays),))],
        compiler_params=pltpu.CompilerParams(vmem_limit_bytes=64 * MIB),
        name="pack",
    )(*arrays)


def attend_kernel(piece, q_ref, r_ref, k_ref, v_ref, dec_ref, mem_ref, out_ref):
    scores = lax.dot_general(
        q_ref[...], k_ref[...], (((1,), (1,)), ((), ())), preferred_element_type=F32
    )
    scores = scores * (1.0 / math.sqrt(HEAD_DIM))
    scores = jnp.where(dec_ref[...] == mem_ref[...], scores, -jnp.inf)
    top = jnp.max(scores, axis=1, keepdims=True)
    raised = jnp.exp(scores - top)
    weights = (raised / jnp.sum(raised, axis=1, keepdims=True)).astype(BF16)
    context = jnp.dot(weights, v_ref[...], preferred_element_type=F32).astype(BF16)
    summed = r_ref[...].astype(F32) + context.astype(F32)
    halves = out_ref.shape[0]
    summed = summed.reshape(-1, halves, piece // halves, HEAD_DIM)
    for half in range(halves):
        out_ref[half] = summed[:, half].reshape(-1, HEAD_DIM).astype(BF16)


def attend(q, r, k, v, dec, mem, piece, halves):
    rows, mem_rows = q.shape[0], k.shape[0]
    tile = 128
    whole = lambda i: (0, 0)
    step = lambda i: (i, 0)

    def kernel(*refs):
        attend_kernel(piece, *refs)

    return pl.pallas_call(
        kernel,
        grid=(rows // tile,),
        in_specs=[
            pl.BlockSpec((tile, HEAD_DIM), step),
            pl.BlockSpec((tile, HEAD_DIM), step),
            pl.BlockSpec((mem_rows, HEAD_DIM), whole),
            pl.BlockSpec((mem_rows, HEAD_DIM), whole),
            pl.BlockSpec((tile, 1), step),
            pl.BlockSpec((1, mem_rows), whole),
        ],
        out_specs=pl.BlockSpec((halves, tile // halves, HEAD_DIM), lambda i: (0, i, 0)),
        out_shape=jax.ShapeDtypeStruct((halves, rows // halves, HEAD_DIM), BF16),
        compiler_params=pltpu.CompilerParams(vmem_limit_bytes=24 * MIB),
        name="attend",
    )(q, r, k, v, dec, mem)


def head_kernel(
    vocab, slabs, places, group, sets, info_ref, gain_ref, bias_ref, t_ref, *rest
):
    out_ref, held, normed, logits, columns, turned, sems = rest[-7:]
    x_refs, w_refs = rest[: -7 - slabs], rest[-7 - slabs : -7]
    copies = [
        pltpu.make_async_copy(w_refs[k], held.at[k], sems.at[k]) for k in range(slabs)
    ]
    for copy in copies:
        copy.start()
    turns = 4
    enc, z, own_rows = (info_ref[slabs + index] for index in range(3))
    halves, rows, chunk = x_refs[0].shape[1:]
    heads = len(places)
    width = w_refs[0].shape[1]
    side = columns.shape[1]
    step = 16
    lane = lax.broadcasted_iota(jnp.int32, (step, side), 1)

    voc_count = t_ref.shape[0]
    share = rows // voc_count
    filler = jnp.zeros((side - voc_count, side), F32)
    turned[...] = jnp.transpose(jnp.concatenate([t_ref[...], filler], axis=0))
    at = pl.multiple_of(lax.rem(z + group, sets) * (side // 2 // sets) + own_rows, share)
    block = turned[pl.ds(at, share)]
    for voc in range(voc_count):
        columns[pl.ds(voc * share, share)] = jnp.broadcast_to(
            block[:, voc : voc + 1], (share, side)
        )

    order = [(place, half) for place in places for half in range(halves)]
    bases = []
    for (_, _, turn, index), half in order:
        head = index * (turns // sets) + lax.rem(z + turn, turns) // sets
        at_half = jnp.where(enc == 0, half, 1 - half)
        bases.append(pl.multiple_of((at_half * heads + head) * chunk, chunk))
    for low in range(0, rows, step):
        at = pl.ds(low, step)
        parts = [x_refs[place[0]][place[1], half, at].astype(F32) for place, half in order]
        mean = jnp.sum(sum(parts[1:], parts[0]), axis=1, keepdims=True) * (1.0 / D)
        parts = [part - mean for part in parts]
        squares = [part * part for part in parts]
        var = jnp.sum(sum(squares[1:], squares[0]), axis=1, keepdims=True) * (1.0 / D)
        scale = lax.rsqrt(var + LN_EPS)
        for base, part in zip(bases, parts):
            lanes = pl.ds(base, chunk)
            value = part * scale * gain_ref[:, lanes] + bias_ref[:, lanes]
            normed[at, lanes] = value.astype(BF16)

    for k in range(slabs):
        copies[k].wait()
        logits[:, pl.ds(k * width, width)] = jnp.dot(
            normed[...], held[k], preferred_element_type=F32
        )

    for low in range(0, rows, step):
        at = pl.ds(low, step)
        target = columns[at].astype(jnp.int32)
        top = logits[at, pl.ds(0, side)]
        for col in range(side, slabs * width, side):
            top = jnp.maximum(top, logits[at, pl.ds(col, side)])
        top = jnp.max(top, axis=1, keepdims=True)
        exps = sums = picks = jnp.zeros((step, side), F32)
        for k in range(slabs):
            offset = target - info_ref[k] - lane
            for col in range(0, width, side):
                part = logits[at, pl.ds(k * width + col, side)]
                exps = exps + jnp.exp(part - top)
                sums = sums + part
                picks = picks + jnp.where(offset == col, part, 0.0)
        lse = top + jnp.log(jnp.sum(exps, axis=1, keepdims=True))
        line = (1.0 - EPS_SMOOTH) * picks + (EPS_SMOOTH / vocab) * sums
        line = jnp.sum(line, axis=1, keepdims=True)
        columns[at] = jnp.where(lane == 0, lse, line)

    for low in range(0, rows, side):
        block = jnp.transpose(columns[pl.ds(low, side)])
        out_ref[:, pl.ds(low, side)] = block[: out_ref.shape[0]]


def head_stats(xs, places, group, sets, gain, bias, targets, slabs, info, vocab):
    rows = xs[0].shape[2]
    width = slabs[0].shape[1]

    def kernel(*refs):
        head_kernel(vocab, len(slabs), places, group, sets, *refs)

    vmem = pl.BlockSpec(memory_space=pltpu.VMEM)
    hbm = pl.BlockSpec(memory_space=pltpu.HBM)
    stats = pl.pallas_call(
        kernel,
        in_specs=[pl.BlockSpec(memory_space=pltpu.SMEM)]
        + [vmem] * (3 + len(xs))
        + [hbm] * len(slabs),
        out_specs=vmem,
        out_shape=jax.ShapeDtypeStruct((8, rows), F32),
        scratch_shapes=[
            pltpu.VMEM((len(slabs), D, width), BF16),
            pltpu.VMEM((rows, D), BF16),
            pltpu.VMEM((rows, len(slabs) * width), F32),
            pltpu.VMEM((rows, 128), F32),
            pltpu.VMEM((128, 128), F32),
            pltpu.SemaphoreType.DMA((len(slabs),)),
        ],
        compiler_params=pltpu.CompilerParams(vmem_limit_bytes=50 * MIB),
        cost_estimate=pl.CostEstimate(
            flops=2 * rows * D * len(slabs) * width,
            bytes_accessed=2 * D * len(slabs) * width,
            transcendentals=rows * len(slabs) * width,
        ),
        name="head_stats",
    )(info, gain, bias, targets, *xs, *slabs)
    return stats[:2]


def per_device(
    queries,
    residual,
    mem_keys,
    mem_values,
    dec_ids,
    mem_ids,
    targets,
    ln_gain,
    ln_bias,
    head_weight,
):
    enc, z, yhi = (lax.axis_index(name) for name in ("enc", Z, "yhi"))
    enc_count, z_count, y_count = (lax.axis_size(name) for name in ("enc", Z, "yhi"))
    voc_count = z_count * y_count
    heads = queries.shape[1] // HEAD_DIM
    parts = voc_count // heads
    sets = parts // y_count
    rows, mem_rows = queries.shape[0], mem_keys.shape[0]
    piece = rows // parts
    slice_rows = piece // enc_count
    width = head_weight.shape[1]
    vocab = width * voc_count * enc_count

    with jax.named_scope("weights"):
        weight_y = lax.ppermute(head_weight, "yhi", SWAP)
        weight_e = lax.ppermute(head_weight, "enc", SWAP)
    with jax.named_scope("pack"):
        message = pack(
            queries, residual, mem_keys, mem_values, dec_ids, mem_ids, targets, parts
        )
    with jax.named_scope("spread"):
        got = lax.all_to_all(message, VOC, 0, 0, tiled=True)
        got, weight_e = lax.optimization_barrier((got, weight_e))
    with jax.named_scope("attention"):
        at_q = 2 * mem_rows
        take = lambda low, count: got[:, low : low + count].reshape(-1, HEAD_DIM)
        noted = got[:, at_q + 2 * piece : at_q + 2 * piece + 4].astype(jnp.int32)
        dec = lax.dynamic_slice_in_dim(
            noted[:, 0, :rows], (z % sets * y_count + yhi) * piece, piece, 1
        ).reshape(-1, 1)
        mem = noted[:, 1, :mem_rows].reshape(1, -1)
        target = (noted[:, 2] * 256 + noted[:, 3]).astype(F32)
        halves = attend(
            take(at_q, piece),
            take(at_q + piece, piece),
            take(0, mem_rows),
            take(mem_rows, mem_rows),
            dec,
            mem,
            piece,
            enc_count,
        )
    with jax.named_scope("halves"):
        kept = lax.dynamic_index_in_dim(halves, enc, 0, False)
        passed = lax.dynamic_index_in_dim(halves, 1 - enc, 0, False)
        shard = jnp.stack([kept, lax.ppermute(passed, "enc", SWAP)])
    with jax.named_scope("rows"):
        up = [(i, (i + 1) % z_count) for i in range(z_count)]
        down = [(i, (i - 1) % z_count) for i in range(z_count)]
        fours = lax.all_gather(shard, "zq", axis=0)
        fours, weight_y = lax.optimization_barrier((fours, weight_y))
        cut = fours.shape[0] // 2
        low, high = fours[:cut], fours[cut:]
        below_low, above_high = lax.ppermute(low, Z, up), lax.ppermute(high, Z, down)
        below_high, above_low = lax.ppermute(high, Z, up), lax.ppermute(low, Z, down)
        far_low, far_high = lax.ppermute(below_low, Z, up), lax.ppermute(above_high, Z, down)
    with jax.named_scope("weights"):
        weight_ye = lax.ppermute(weight_y, "enc", SWAP)
    with jax.named_scope("head"):
        slab = lambda e, y: ((e * voc_count) + z * y_count + y) * width
        info = jnp.stack(
            [
                slab(enc, yhi),
                slab(1 - enc, yhi),
                slab(enc, 1 - yhi),
                slab(1 - enc, 1 - yhi),
                enc,
                z,
                yhi * piece + enc * slice_rows,
            ]
        ).astype(jnp.int32)
        halved = lambda ref, turn, first: [
            (ref, index, turn, first + index) for index in range(cut)
        ]

        def head(group, xs, places):
            found = head_stats(
                xs,
                places,
                group,
                sets,
                ln_gain[None],
                ln_bias[None],
                target,
                (head_weight, weight_e, weight_y, weight_ye),
                info,
                vocab,
            )
            return found.reshape(2, 1, voc_count, slice_rows)

        other = head(
            1,
            [above_low, above_high, below_low, below_high],
            halved(0, 1, 0) + halved(1, 1, cut) + halved(2, 3, 0) + halved(3, 3, cut),
        )
        same = head(
            0,
            [fours, far_low, far_high],
            [(0, index, 0, index) for index in range(2 * cut)]
            + halved(1, 2, 0)
            + halved(2, 2, cut),
        )
        stats = jnp.where(
            z % sets == 0,
            jnp.concatenate([same, other], axis=1),
            jnp.concatenate([other, same], axis=1),
        )
    with jax.named_scope("merge"):
        stats = stats.transpose(2, 0, 1, 3)
        stats = jnp.broadcast_to(
            stats.reshape(1, voc_count, 2, -1), (enc_count, voc_count, 2, sets * slice_rows)
        )
        merged = lax.all_to_all(
            stats.reshape(enc_count * voc_count, 2, -1), ("enc",) + VOC, 0, 0, tiled=True
        )
        merged = merged.reshape(enc_count, z_count, y_count, 2, sets, slice_rows)
        lse, line = merged[:, :, :, 0], merged[:, :, :, 1]
        top = jnp.max(lse, axis=1, keepdims=True)
        log_total = top[:, 0] + jnp.log(jnp.sum(jnp.exp(lse - top), axis=1))
        loss = log_total - jnp.sum(line, axis=1) + Z_COEF * log_total * log_total
        return loss.transpose(2, 1, 0, 3).reshape(rows)


def solution(mesh):
    shape = dict(mesh.shape)
    fine = Mesh(
        mesh.devices.reshape(shape["enc"], shape["blk"], shape["voc"] // 8, 4, 2),
        ("enc", "blk") + VOC,
    )
    held = ("blk",) + VOC
    in_specs = (
        P(held, "enc"),
        P(held, "enc"),
        P(held, "enc"),
        P(held, "enc"),
        P(held),
        P(held),
        P(held),
        P(),
        P(),
        P(None, ("enc",) + VOC),
    )
    return jax.shard_map(
        per_device, mesh=fine, in_specs=in_specs, out_specs=P(held), check_vma=False
    )
```
